512 devices in a mesh: space: 64 (over z, x, core), years: 8 (over y).
Axes of the slice: x: 4, y: 8, z: 8, core: 2. Of those that a mesh axis runs over, the one named last changes fastest.
Arguments:
- maxima: float32 [32, 8, 1024, 640], P('years', None, 'space'), as said below
- fields: float32 [3, 1024, 640], P(None, 'space'), may hold values from -0.7 to 2, as said below
- kappa_sq: float32 [3, 1024, 640], P(None, 'space'), may hold values from 0.05 to 0.4
- anisotropy: float32 [3, 2], replicated, may hold values from 0.05 to 0.15
- precision: float32 [3], replicated, may hold values from 4 to 40
- ocean_mask: int32 [1024, 640], P('space'), may hold values from 0 to 1, as said below
- year_valid: int32 [32], P('years'), may hold values from 0 to 1, as said below
- counts: int32 [1024, 640], P('space'), may hold values from 1 to 8
Outputs:
- gradient: float32 [3, 1024, 640], P(None, 'space')
The draws below stay inside these ranges and needn't reach their ends.
Inputs may be any that keep to these rules, and one draw needn't show every extreme that they name: `maxima`: for each year and cell the values fall strictly with the order. fields[0] lies in 1 to 2, fields[1] in -0.7 to 0, fields[2] in 0.1 to 0.3. `ocean_mask`: every cell of latitude 640 // 2 is ocean. `year_valid`: the last year is valid, and at least one other year is padded.
All inputs are finite; a program needn't handle non-finite values.
Results may differ from the reference program's by a relative error of at most 0.0003.
Values sent between devices are 32-bit elements; how exact they have to be, the bound alone decides.
No kernel may reach another device: no remote copies, remote signals or barrier semaphores. Data moves between devices by JAX's collectives and lax.ppermute only.
A program may use at most 64 MiB of HBM per device.

```python
import math
import jax
import jax.numpy as jnp
from jax import lax

NLAT = 640
R = 8
SWEEPS = 8
NLON = 1024
YEARS = 32


def draw_maxima(key, part):
    first_key, second_key, third_key = jax.random.split(key, 3)
    uniform_draw = jax.random.uniform(first_key, (YEARS, 1, NLON, NLAT), jnp.float32)
    base_level = 2.5 * uniform_draw
    spacing = 0.05 + 0.35 * jax.random.uniform(second_key, (YEARS, 1, NLON, NLAT), jnp.float32)
    jitter = 0.9 * spacing * jax.random.uniform(third_key, (YEARS, R, NLON, NLAT), jnp.float32)
    order_index = jnp.arange(R).reshape(1, R, 1, 1).astype(jnp.float32)
    return 1.6 + base_level + spacing * (R - 1 - order_index) + jitter


def draw_fields(key, part):
    uniform_draw = jax.random.uniform(key, (3, NLON, NLAT), jnp.float32)
    lower = jnp.array([1.0, -0.7, 0.1], jnp.float32)[:, None, None]
    upper = jnp.array([2.0, 0.0, 0.3], jnp.float32)[:, None, None]
    return lower + (upper - lower) * uniform_draw


def draw_ocean_mask(key, part):
    random_ints = jax.random.randint(key, (NLON, NLAT), 0, 4 * NLON)
    column_index = jnp.arange(NLON, dtype=jnp.int32)[:, None]
    row_index = jnp.arange(NLAT, dtype=jnp.int32)[None, :]
    ocean = (random_ints < NLON + 2 * column_index) | (row_index == NLAT // 2)
    return ocean.astype(jnp.int32)


def draw_year_valid(key, part):
    key = jax.random.fold_in(key, 11)
    first_key, second_key = jax.random.split(key, 2)
    random_ints = jax.random.randint(first_key, (YEARS,), 0, 10)
    padded_year = jax.random.randint(second_key, (), 0, YEARS - 1)
    year_index = jnp.arange(YEARS, dtype=jnp.int32)
    valid = (random_ints < 6) | (year_index == YEARS - 1)
    valid = valid & (year_index != padded_year)
    return valid.astype(jnp.int32)


def place_ends(values, rng, smallest, high):
    index_at = [jax.random.randint(jax.random.fold_in(rng, axis), (), 0, length) for axis, length in enumerate(values.shape)]
    longest = values.shape.index(max(values.shape))
    beside = index_at[:longest] + [(index_at[longest] + 1) % values.shape[longest]] + index_at[longest + 1:]
    return values.at[tuple(index_at)].set(smallest).at[tuple(beside)].set(high)


def level_of(key, shape, cuts, smallest, largest):
    level, own = 1.0, jax.random.fold_in(key, 6)
    for position, blocks in cuts:
        heights = jnp.exp(jax.random.uniform(jax.random.fold_in(own, position), (blocks,), jnp.float32, smallest / len(cuts), largest / len(cuts)))
        level = level * jnp.repeat(heights, shape[position] // blocks).reshape([-1 if axis == position else 1 for axis in range(len(shape))])
    return level


def setup_inputs(seed: int = 0) -> dict:
    seeds = jax.random.split(jax.random.key(seed), 9)
    maxima = draw_maxima(jax.random.fold_in(seeds[8], 71), 0)
    fields = draw_fields(jax.random.fold_in(seeds[8], 71), 0)
    kappa_sq = jnp.clip(jnp.exp(math.log(0.4) - 2.0794415 * jax.random.uniform(seeds[2], (3, NLON, NLAT), jnp.float32) ** level_of(seeds[2], (3, NLON, NLAT), ((1, 64),), -0.2, 0.2)), 0.05, 0.4)
    anisotropy = jnp.clip(jax.random.uniform(seeds[3], (3, 2), jnp.float32, 0.05, 0.15), 0.05, 0.15)
    precision = jnp.clip(jnp.exp(jax.random.uniform(seeds[4], (3,), jnp.float32, math.log(4.0), math.log(40.0))), 4.0, 40.0)
    ocean_mask = draw_ocean_mask(jax.random.fold_in(seeds[8], 71), 0)
    year_valid = draw_year_valid(jax.random.fold_in(seeds[8], 71), 0)
    counts = place_ends(jax.random.randint(seeds[7], (NLON, NLAT), 1, R + 1), jax.random.fold_in(seeds[7], 1), 1, R).astype(jnp.int32)
    return {"maxima": maxima, "fields": fields, "kappa_sq": kappa_sq, "anisotropy": anisotropy, "precision": precision, "ocean_mask": ocean_mask, "year_valid": year_valid, "counts": counts}


def apply_operator(values, kappa_sq, anisotropy):
    zonal_weight = anisotropy[:, 0][:, None, None]
    meridional_weight = anisotropy[:, 1][:, None, None]
    east_west = jnp.roll(values, 1, axis=1) + jnp.roll(values, -1, axis=1)
    padded = jnp.pad(values, ((0, 0), (0, 0), (1, 1)))
    north_south = padded[:, :, 2:] + padded[:, :, :-2]
    return (kappa_sq + 2.0 * zonal_weight + 2.0 * meridional_weight) * values - zonal_weight * east_west - meridional_weight * north_south

def year_loss(fields, year_maxima, valid, ocean_mask, counts):
    location = fields[0]
    log_scale = fields[1]
    tail_shape = fields[2]
    reduced = 1.0 + tail_shape * (year_maxima - location) / jnp.exp(log_scale)
    log_reduced = jnp.log(reduced)
    order_index = jnp.arange(R, dtype=jnp.int32)[:, None, None]
    order_used = order_index < counts[None]
    order_last = order_index == counts[None] - 1
    tail_term = jnp.exp(-lax.optimization_barrier(jnp.sum(jnp.where(order_last, log_reduced, 0.0), axis=0)) / tail_shape)
    order_terms = lax.optimization_barrier(jnp.sum(jnp.where(order_used, log_scale + (1.0 + 1.0 / tail_shape) * log_reduced, 0.0), axis=0))
    weight = (ocean_mask * valid).astype(jnp.float32)
    return jnp.sum(weight * (tail_term + order_terms))

def reference(maxima, fields, kappa_sq, anisotropy, precision, ocean_mask, year_valid, counts):
    year_gradient = jax.grad(year_loss)

    def accumulate(summed, year_item):
        year_maxima, valid = year_item
        return (summed + year_gradient(fields, year_maxima, valid, ocean_mask, counts), None)
    summed, _ = lax.scan(accumulate, jnp.zeros_like(fields), (maxima, year_valid))
    cell_count = jnp.sum(ocean_mask * counts).astype(jnp.float32)
    year_count = jnp.sum(year_valid).astype(jnp.float32)
    observations = cell_count * year_count
    likelihood_grad = summed * (jnp.float32(NLON * NLAT) / observations)
    values = fields
    for sweep_index in range(SWEEPS):
        values = apply_operator(values, kappa_sq, anisotropy)
    return likelihood_grad + precision[:, None, None] * values
```

```python
import jax
import jax.numpy as jnp
from jax import lax
from jax.experimental import pallas as pl
from jax.experimental.pallas import tpu as pltpu
from jax.sharding import PartitionSpec as P

SWEEPS = 8
HALO = 8
LANES = 128
SUB = 8
VMEM = pl.BlockSpec(memory_space=pltpu.VMEM)
SMEM = pl.BlockSpec(memory_space=pltpu.SMEM)


def likelihood_kernel(
    valid_ref, maxima_ref, fields_ref, kappa_ref, mask_ref, counts_ref,
    tiles_ref, cells_ref, low_ref, high_ref,
):
    years, orders, rows, columns = maxima_ref.shape
    row_tiles, lane_tiles = rows // SUB, columns // LANES
    valid = [valid_ref[t].astype(jnp.float32) for t in range(years)]
    valid_sum = sum(valid[1:], valid[0])
    cells = jnp.zeros((SUB, LANES), jnp.float32)
    for r in range(row_tiles):
        for c in range(lane_tiles):
            at = (pl.ds(r * SUB, SUB), pl.ds(c * LANES, LANES))
            location = fields_ref[(0,) + at]
            log_scale = fields_ref[(1,) + at]
            shape = fields_ref[(2,) + at]
            count = counts_ref[at]
            mask = mask_ref[at].astype(jnp.float32)
            inv_scale = jnp.exp(-log_scale)
            inv_shape = 1.0 / shape
            slope = shape * inv_scale
            sum_inv = jnp.zeros((SUB, LANES), jnp.float32)
            sum_log = jnp.zeros((SUB, LANES), jnp.float32)
            tail_sum = jnp.zeros((SUB, LANES), jnp.float32)
            tail_inv = jnp.zeros((SUB, LANES), jnp.float32)
            tail_log = jnp.zeros((SUB, LANES), jnp.float32)
            for t in range(years):
                inv_t = None
                for k in range(orders):
                    reduced = 1.0 + slope * (maxima_ref[(t, k) + at] - location)
                    if k == 0:
                        used, last = reduced, reduced
                    else:
                        is_used = count > k
                        used = jnp.where(is_used, reduced, 1.0)
                        last = jnp.where(is_used, reduced, last)
                    inv = 1.0 - 1.0 / used
                    log = jnp.log(used)
                    if k == 0:
                        inv_t, log_t = inv, log
                    else:
                        inv_t, log_t = inv_t + inv, log_t + log
                last_log = jnp.log(last)
                tail = jnp.exp(-last_log * inv_shape) * valid[t]
                sum_inv = sum_inv + inv_t * valid[t]
                sum_log = sum_log + log_t * valid[t]
                tail_sum = tail_sum + tail
                tail_inv = tail_inv + tail / last
                tail_log = tail_log + tail * last_log
            used_total = valid_sum * count.astype(jnp.float32)
            one_more = 1.0 + inv_shape
            tail_diff = tail_sum - tail_inv
            grad = (
                (tail_inv - (1.0 + shape) * (used_total - sum_inv)) * inv_scale,
                used_total - one_more * sum_inv + tail_diff * inv_shape,
                (
                    (tail_log - sum_log - tail_diff) * inv_shape
                    + one_more * sum_inv
                ) * inv_shape,
            )
            for f in range(3):
                tiles_ref[(f * row_tiles + r) * lane_tiles + c] = grad[f] * mask
            cells = cells + mask * count.astype(jnp.float32)
    used_tiles = 3 * row_tiles * lane_tiles
    tiles_ref[used_tiles] = jnp.full((SUB, LANES), valid_sum, jnp.float32)
    for q in range(used_tiles + 1, tiles_ref.shape[0]):
        tiles_ref[q] = jnp.zeros((SUB, LANES), jnp.float32)
    cells_ref[...] = jnp.broadcast_to(
        jnp.sum(cells, axis=0, keepdims=True), cells_ref.shape
    )
    low_ref[0:3] = fields_ref[:, 0:HALO]
    low_ref[3:6] = kappa_ref[:, 0:HALO]
    high_ref[0:3] = fields_ref[:, rows - HALO : rows]
    high_ref[3:6] = kappa_ref[:, rows - HALO : rows]


def middle_kernel(parts_ref, out_ref):
    groups = parts_ref.shape[0]
    total = parts_ref[0]
    for g in range(1, groups):
        total = total + parts_ref[g]
    for g in range(groups):
        out_ref[g] = total


def prior_kernel(aniso_ref, precision_ref, fields_ref, kappa_ref, low_ref, high_ref, out_ref):
    rows, columns = fields_ref.shape[1:]
    extent = rows + 2 * HALO
    lane = lax.broadcasted_iota(jnp.int32, (extent, columns), 1)
    for f in range(3):
        zonal, meridional = aniso_ref[f, 0], aniso_ref[f, 1]
        values = jnp.concatenate([low_ref[f], fields_ref[f], high_ref[f]], axis=0)
        centre = jnp.concatenate([low_ref[3 + f], kappa_ref[f], high_ref[3 + f]], axis=0)
        centre = centre + (2.0 * zonal + 2.0 * meridional)
        for _ in range(SWEEPS):
            east_west = pltpu.roll(values, 1, 0) + pltpu.roll(values, extent - 1, 0)
            south = jnp.where(lane == 0, 0.0, pltpu.roll(values, 1, 1))
            north = jnp.where(lane == columns - 1, 0.0, pltpu.roll(values, columns - 1, 1))
            values = centre * values - zonal * east_west - meridional * (south + north)
        out_ref[f] = precision_ref[f] * values[HALO : HALO + rows]


def final_kernel(grid_cells, tiles_ref, cells_ref, prior_ref, out_ref):
    rows, columns = out_ref.shape[1:]
    row_tiles, lane_tiles = rows // SUB, columns // LANES
    cell_count = jnp.sum(
        jnp.sum(cells_ref[...], axis=0, keepdims=True), axis=1, keepdims=True
    )
    year_count = tiles_ref[3 * row_tiles * lane_tiles, 0:1, 0:1]
    scale = jnp.broadcast_to(grid_cells / (cell_count * year_count), (SUB, LANES))
    for f in range(3):
        for r in range(row_tiles):
            for c in range(lane_tiles):
                at = (f, pl.ds(r * SUB, SUB), pl.ds(c * LANES, LANES))
                tile = tiles_ref[(f * row_tiles + r) * lane_tiles + c]
                out_ref[at] = tile * scale + prior_ref[at]


def shifted(axis, step):
    count = lax.axis_size(axis)
    return [(i, (i + step) % count) for i in range(count)]


def local(maxima, fields, kappa_sq, anisotropy, precision, ocean_mask, year_valid, counts):
    f32 = jnp.float32
    rows, columns = fields.shape[1:]
    spaces, groups = lax.axis_size("space"), lax.axis_size("years")
    used_tiles = 3 * (rows // SUB) * (columns // LANES) + 1
    tile_count = -(-used_tiles // groups) * groups
    tiles_shape = jax.ShapeDtypeStruct((tile_count, SUB, LANES), f32)
    halo_shape = jax.ShapeDtypeStruct((6, HALO, columns), f32)
    tiles, cells, low, high = pl.pallas_call(
        likelihood_kernel,
        out_shape=(tiles_shape, jax.ShapeDtypeStruct((spaces, LANES), f32), halo_shape, halo_shape),
        in_specs=[SMEM] + [VMEM] * 5,
        out_specs=(VMEM,) * 4,
        cost_estimate=pl.CostEstimate(
            flops=20 * maxima.size, bytes_accessed=4 * maxima.size, transcendentals=2 * maxima.size
        ),
        name="likelihood",
    )(year_valid, maxima, fields, kappa_sq, ocean_mask, counts)

    parts = lax.all_to_all(tiles, "years", 0, 0, tiled=True)
    from_low = lax.ppermute(high, "space", shifted("space", 1))
    from_high = lax.ppermute(low, "space", shifted("space", -1))
    cell_parts = lax.all_to_all(cells, "space", 0, 0, tiled=True)

    spread = pl.pallas_call(
        middle_kernel,
        out_shape=jax.ShapeDtypeStruct((groups, tile_count // groups, SUB, LANES), f32),
        in_specs=[VMEM],
        out_specs=VMEM,
        cost_estimate=pl.CostEstimate(flops=tiles.size, bytes_accessed=8 * tiles.size, transcendentals=0),
        name="middle",
    )(parts.reshape(groups, tile_count // groups, SUB, LANES))
    summed = lax.all_to_all(
        spread.reshape(tile_count, SUB, LANES), "years", 0, 0, tiled=True
    )

    prior = pl.pallas_call(
        prior_kernel,
        out_shape=jax.ShapeDtypeStruct(fields.shape, f32),
        in_specs=[SMEM, SMEM] + [VMEM] * 4,
        out_specs=VMEM,
        cost_estimate=pl.CostEstimate(
            flops=20 * SWEEPS * fields.size, bytes_accessed=20 * fields.size, transcendentals=0
        ),
        name="prior",
    )(anisotropy, precision, fields, kappa_sq, from_low, from_high)

    grid_cells = float(rows * spaces * columns)
    return pl.pallas_call(
        lambda *refs: final_kernel(grid_cells, *refs),
        out_shape=jax.ShapeDtypeStruct(fields.shape, f32),
        in_specs=[VMEM] * 3,
        out_specs=VMEM,
        cost_estimate=pl.CostEstimate(flops=2 * fields.size, bytes_accessed=12 * fields.size, transcendentals=0),
        name="final",
    )(summed, cell_parts, prior)


def solution(mesh):
    return jax.shard_map(
        local,
        mesh=mesh,
        in_specs=(
            P("years", None, "space", None),
            P(None, "space", None),
            P(None, "space", None),
            P(),
            P(),
            P("space", None),
            P("years"),
            P("space", None),
        ),
        out_specs=P(None, "space", None),
        check_vma=False,
    )
```

```python
import jax
import jax.numpy as jnp
from jax import lax
from jax.experimental import pallas as pl
from jax.experimental.pallas import tpu as pltpu
from jax.sharding import PartitionSpec as P

SWEEPS = 8
HALO = 8
LANES = 128
SUB = 8
MIB = 1 << 20
PIECE = 4
WIDE = 96
CELL_LANE = 96
YEAR_LANE = 97
VMEM = pl.BlockSpec(memory_space=pltpu.VMEM)
SMEM = pl.BlockSpec(memory_space=pltpu.SMEM)


def packed_tiles(tiles, spare):
    lane = lax.broadcasted_iota(jnp.int32, (SUB, LANES), 1)
    packed = list(tiles[:24])
    packed += [jnp.where(lane < WIDE, tile, spare) for tile in tiles[24:]]
    for i in (24, 27):
        rolled = [pltpu.roll(tiles[i + j], 32 * (j + 1), 1) for j in range(3)]
        rest = jnp.where(lane < 32, rolled[0], jnp.where(lane < 64, rolled[1], rolled[2]))
        packed.append(jnp.where(lane < WIDE, rest, spare))
    return packed


def unpacked_tiles(packed):
    lane = lax.broadcasted_iota(jnp.int32, (SUB, LANES), 1)
    tiles = list(packed[:24])
    for i in range(6):
        rest = pltpu.roll(packed[30 + i // 3], 96 - 32 * (i % 3), 1)
        tiles.append(jnp.where(lane < WIDE, packed[24 + i], rest))
    return tiles


def place(q):
    row, group = (q % 3, q // 3) if q < 24 else (3, q - 24)
    return pl.ds(group * SUB * PIECE + row, SUB, PIECE)


def likelihood_kernel(
    valid_ref, maxima_ref, fields_ref, kappa_ref, mask_ref, counts_ref,
    packed_ref, cells_ref, low_ref, high_ref,
):
    years, orders, rows, columns = maxima_ref.shape
    row_tiles, lane_tiles = rows // SUB, columns // LANES
    valid = [valid_ref[t].astype(jnp.float32) for t in range(years)]
    valid_sum = sum(valid[1:], valid[0])
    cells = jnp.zeros((SUB, LANES), jnp.float32)
    tiles = [None] * (3 * row_tiles * lane_tiles)
    for r in range(row_tiles):
        for c in range(lane_tiles):
            at = (pl.ds(r * SUB, SUB), pl.ds(c * LANES, LANES))
            location = fields_ref[(0,) + at]
            log_scale = fields_ref[(1,) + at]
            shape = fields_ref[(2,) + at]
            count = counts_ref[at]
            mask = mask_ref[at].astype(jnp.float32)
            inv_scale = jnp.exp(-log_scale)
            inv_shape = 1.0 / shape
            slope = shape * inv_scale
            sum_inv = jnp.zeros((SUB, LANES), jnp.float32)
            sum_log = jnp.zeros((SUB, LANES), jnp.float32)
            tail_sum = jnp.zeros((SUB, LANES), jnp.float32)
            tail_inv = jnp.zeros((SUB, LANES), jnp.float32)
            tail_log = jnp.zeros((SUB, LANES), jnp.float32)
            for t in range(years):
                inv_t = None
                for k in range(orders):
                    reduced = 1.0 + slope * (maxima_ref[(t, k) + at] - location)
                    if k == 0:
                        used, last = reduced, reduced
                    else:
                        is_used = count > k
                        used = jnp.where(is_used, reduced, 1.0)
                        last = jnp.where(is_used, reduced, last)
                    inv = 1.0 - 1.0 / used
                    log = jnp.log(used)
                    if k == 0:
                        inv_t, log_t = inv, log
                    else:
                        inv_t, log_t = inv_t + inv, log_t + log
                last_log = jnp.log(last)
                tail = jnp.exp(-last_log * inv_shape) * valid[t]
                sum_inv = sum_inv + inv_t * valid[t]
                sum_log = sum_log + log_t * valid[t]
                tail_sum = tail_sum + tail
                tail_inv = tail_inv + tail / last
                tail_log = tail_log + tail * last_log
            used_total = valid_sum * count.astype(jnp.float32)
            one_more = 1.0 + inv_shape
            tail_diff = tail_sum - tail_inv
            grad = (
                (tail_inv - (1.0 + shape) * (used_total - sum_inv)) * inv_scale,
                used_total - one_more * sum_inv + tail_diff * inv_shape,
                (
                    (tail_log - sum_log - tail_diff) * inv_shape
                    + one_more * sum_inv
                ) * inv_shape,
            )
            for f in range(3):
                tiles[(f * row_tiles + r) * lane_tiles + c] = grad[f] * mask
            cells = cells + mask * count.astype(jnp.float32)
    lane = lax.broadcasted_iota(jnp.int32, (SUB, LANES), 1)
    spare = jnp.where(lane == YEAR_LANE, valid_sum, 0.0)
    for q, tile in enumerate(packed_tiles(tiles, spare)):
        packed_ref[place(q), :] = tile
    cell_sum = jnp.sum(jnp.sum(cells, axis=0, keepdims=True), axis=1, keepdims=True)
    row = lax.broadcasted_iota(jnp.int32, (PIECE, LANES), 0)
    lane = lax.broadcasted_iota(jnp.int32, (PIECE, LANES), 1)
    cells_ref[...] = jnp.where((row == PIECE - 1) & (lane == CELL_LANE), cell_sum, 0.0)
    low_ref[0:3] = fields_ref[:, 0:HALO]
    low_ref[3:6] = kappa_ref[:, 0:HALO]
    high_ref[0:3] = fields_ref[:, rows - HALO : rows]
    high_ref[3:6] = kappa_ref[:, rows - HALO : rows]


def prior_kernel(aniso_ref, precision_ref, fields_ref, kappa_ref, low_ref, high_ref, out_ref):
    rows, columns = fields_ref.shape[1:]
    extent = rows + 2 * HALO
    lane = lax.broadcasted_iota(jnp.int32, (extent, columns), 1)
    for f in range(3):
        zonal, meridional = aniso_ref[0, f], aniso_ref[1, f]
        values = jnp.concatenate([low_ref[f], fields_ref[f], high_ref[f]], axis=0)
        centre = jnp.concatenate([low_ref[3 + f], kappa_ref[f], high_ref[3 + f]], axis=0)
        centre = centre + (2.0 * zonal + 2.0 * meridional)
        for _ in range(SWEEPS):
            east_west = pltpu.roll(values, 1, 0) + pltpu.roll(values, extent - 1, 0)
            south = jnp.where(lane == 0, 0.0, pltpu.roll(values, 1, 1))
            north = jnp.where(lane == columns - 1, 0.0, pltpu.roll(values, columns - 1, 1))
            values = centre * values - zonal * east_west - meridional * (south + north)
        out_ref[f] = precision_ref[f] * values[HALO : HALO + rows]


def final_kernel(grid_cells, packed_ref, prior_ref, out_ref):
    rows, columns = out_ref.shape[1:]
    row_tiles, lane_tiles = rows // SUB, columns // LANES
    packed = [packed_ref[place(q), :] for q in range(32)]
    spare = packed[24]
    for tile in packed[25:]:
        spare = spare + tile
    spare = jnp.sum(spare, axis=0, keepdims=True)
    lane = lax.broadcasted_iota(jnp.int32, spare.shape, 1)
    cell_count = jnp.sum(jnp.where(lane == CELL_LANE, spare, 0.0), axis=1, keepdims=True)
    years = jnp.where(lane == YEAR_LANE, packed[24][0:1], 0.0)
    year_count = jnp.sum(years, axis=1, keepdims=True)
    scale = jnp.broadcast_to(grid_cells / (cell_count * year_count), (SUB, LANES))
    tiles = unpacked_tiles(packed)
    for f in range(3):
        for r in range(row_tiles):
            for c in range(lane_tiles):
                at = (f, pl.ds(r * SUB, SUB), pl.ds(c * LANES, LANES))
                tile = tiles[(f * row_tiles + r) * lane_tiles + c]
                out_ref[at] = tile * scale + prior_ref[at]


def shifted(axis, step):
    count = lax.axis_size(axis)
    return [(i, (i + step) % count) for i in range(count)]


def local(maxima, fields, kappa_sq, anisotropy, precision, ocean_mask, year_valid, counts):
    f32 = jnp.float32
    rows, columns = fields.shape[1:]
    spaces, groups = lax.axis_size("space"), lax.axis_size("years")
    members = 8 * groups
    planes = [[z * members + m for m in range(members)] for z in range(spaces // 8)]
    halo_shape = jax.ShapeDtypeStruct((6, HALO, columns), f32)
    packed, cells, low, high = pl.pallas_call(
        likelihood_kernel,
        out_shape=(
            jax.ShapeDtypeStruct((members * PIECE, LANES), f32),
            jax.ShapeDtypeStruct((PIECE, LANES), f32),
            halo_shape,
            halo_shape,
        ),
        in_specs=[SMEM] + [VMEM] * 5,
        out_specs=(VMEM,) * 4,
        cost_estimate=pl.CostEstimate(
            flops=20 * maxima.size, bytes_accessed=4 * maxima.size, transcendentals=2 * maxima.size
        ),
        name="likelihood",
    )(year_valid, maxima, fields, kappa_sq, ocean_mask, counts)

    def exchange(pieces):
        return lax.all_to_all(
            pieces, ("space", "years"), 0, 0, tiled=True, axis_index_groups=planes
        )

    parts = exchange(packed.reshape(members, PIECE, LANES))
    far = [
        (((z + y) % 8 * 8 + a) * groups + y, (z * 8 + a) * groups + y)
        for z in range(8)
        for a in range(8)
        for y in range(groups)
    ]
    far_cells = lax.ppermute(cells, ("space", "years"), far)
    summed = jnp.sum(parts.reshape(8, groups, PIECE, LANES), axis=1) + far_cells
    spread = jnp.broadcast_to(summed[:, None], (8, groups, PIECE, LANES))
    spread, low, high = lax.optimization_barrier((spread, low, high))
    from_low = lax.ppermute(high, "space", shifted("space", 1))
    from_high = lax.ppermute(low, "space", shifted("space", -1))
    whole = exchange(spread.reshape(members, PIECE, LANES))

    prior = pl.pallas_call(
        prior_kernel,
        out_shape=jax.ShapeDtypeStruct(fields.shape, f32),
        in_specs=[SMEM, SMEM] + [VMEM] * 4,
        out_specs=VMEM,
        cost_estimate=pl.CostEstimate(
            flops=20 * SWEEPS * fields.size, bytes_accessed=20 * fields.size, transcendentals=0
        ),
        compiler_params=pltpu.CompilerParams(vmem_limit_bytes=6 * MIB),
        name="prior",
    )(anisotropy.T, precision, fields, kappa_sq, from_low, from_high)

    grid_cells = float(rows * spaces * columns)
    return pl.pallas_call(
        lambda *refs: final_kernel(grid_cells, *refs),
        out_shape=jax.ShapeDtypeStruct(fields.shape, f32),
        in_specs=[VMEM] * 2,
        out_specs=VMEM,
        cost_estimate=pl.CostEstimate(flops=2 * fields.size, bytes_accessed=12 * fields.size, transcendentals=0),
        compiler_params=pltpu.CompilerParams(vmem_limit_bytes=3 * MIB),
        name="final",
    )(whole.reshape(members * PIECE, LANES), prior)


def solution(mesh):
    return jax.shard_map(
        local,
        mesh=mesh,
        in_specs=(
            P("years", None, "space", None),
            P(None, "space", None),
            P(None, "space", None),
            P(),
            P(),
            P("space", None),
            P("years"),
            P("space", None),
        ),
        out_specs=P(None, "space", None),
        check_vma=False,
    )
```

```python
import jax
import jax.numpy as jnp
from jax import lax
from jax.experimental import pallas as pl
from jax.experimental.pallas import tpu as pltpu
from jax.sharding import PartitionSpec as P

SWEEPS = 8
HALO = 8
LANES = 128
SUB = 8
MIB = 1 << 20
PIECE = 32
CELL_ROW = 30
YEAR_ROW = 31
VMEM = pl.BlockSpec(memory_space=pltpu.VMEM)
SMEM = pl.BlockSpec(memory_space=pltpu.SMEM)


def place(q):
    if q < 24:
        return pl.ds(q // 3 * PIECE + q % 3 * SUB, SUB)
    return pl.ds(q, SUB, PIECE)


def cells_kernel(mask_ref, counts_ref, cells_ref):
    rows, columns = mask_ref.shape
    total = jnp.zeros((SUB, LANES), jnp.int32)
    for r in range(0, rows, SUB):
        for c in range(0, columns, LANES):
            at = (pl.ds(r, SUB), pl.ds(c, LANES))
            total = total + mask_ref[at] * counts_ref[at]
    total = jnp.sum(total.astype(jnp.float32), axis=0, keepdims=True)
    cells_ref[...] = jnp.broadcast_to(total, cells_ref.shape)


def likelihood_kernel(
    odd_ref, valid_ref, maxima_ref, fields_ref, kappa_ref, mask_ref, counts_ref,
    packed_ref, inner_ref, outer_ref,
):
    years, orders, rows, columns = maxima_ref.shape
    row_tiles, lane_tiles = rows // SUB, columns // LANES
    valid = [valid_ref[t].astype(jnp.float32) for t in range(years)]
    valid_sum = sum(valid[1:], valid[0])
    tiles = [None] * (3 * row_tiles * lane_tiles)
    for r in range(row_tiles):
        for c in range(lane_tiles):
            at = (pl.ds(r * SUB, SUB), pl.ds(c * LANES, LANES))
            location = fields_ref[(0,) + at]
            log_scale = fields_ref[(1,) + at]
            shape = fields_ref[(2,) + at]
            count = counts_ref[at]
            mask = mask_ref[at].astype(jnp.float32)
            inv_scale = jnp.exp(-log_scale)
            inv_shape = 1.0 / shape
            slope = shape * inv_scale
            sum_inv = jnp.zeros((SUB, LANES), jnp.float32)
            sum_log = jnp.zeros((SUB, LANES), jnp.float32)
            tail_sum = jnp.zeros((SUB, LANES), jnp.float32)
            tail_inv = jnp.zeros((SUB, LANES), jnp.float32)
            tail_log = jnp.zeros((SUB, LANES), jnp.float32)
            for t in range(years):
                inv_t = None
                for k in range(orders):
                    reduced = 1.0 + slope * (maxima_ref[(t, k) + at] - location)
                    if k == 0:
                        used, last = reduced, reduced
                    else:
                        is_used = count > k
                        used = jnp.where(is_used, reduced, 1.0)
                        last = jnp.where(is_used, reduced, last)
                    inv = 1.0 - 1.0 / used
                    log = jnp.log(used)
                    if k == 0:
                        inv_t, log_t = inv, log
                    else:
                        inv_t, log_t = inv_t + inv, log_t + log
                last_log = jnp.log(last)
                tail = jnp.exp(-last_log * inv_shape) * valid[t]
                sum_inv = sum_inv + inv_t * valid[t]
                sum_log = sum_log + log_t * valid[t]
                tail_sum = tail_sum + tail
                tail_inv = tail_inv + tail / last
                tail_log = tail_log + tail * last_log
            used_total = valid_sum * count.astype(jnp.float32)
            one_more = 1.0 + inv_shape
            tail_diff = tail_sum - tail_inv
            grad = (
                (tail_inv - (1.0 + shape) * (used_total - sum_inv)) * inv_scale,
                used_total - one_more * sum_inv + tail_diff * inv_shape,
                (
                    (tail_log - sum_log - tail_diff) * inv_shape
                    + one_more * sum_inv
                ) * inv_shape,
            )
            for f in range(3):
                tiles[(f * row_tiles + r) * lane_tiles + c] = grad[f] * mask
    for q, tile in enumerate(tiles):
        packed_ref[place(q), :] = tile
    packed_ref[pl.ds(CELL_ROW, SUB, PIECE), :] = jnp.zeros((SUB, LANES), jnp.float32)
    packed_ref[pl.ds(YEAR_ROW, SUB, PIECE), :] = jnp.full((SUB, LANES), valid_sum, jnp.float32)
    inner_row = pl.multiple_of((1 - odd_ref[0]) * (rows - HALO), HALO)
    outer_row = pl.multiple_of(odd_ref[0] * (rows - HALO), HALO)
    inner_ref[0:3] = fields_ref[:, pl.ds(inner_row, HALO)]
    inner_ref[3:6] = kappa_ref[:, pl.ds(inner_row, HALO)]
    outer_ref[0:3] = fields_ref[:, pl.ds(outer_row, HALO)]
    outer_ref[3:6] = kappa_ref[:, pl.ds(outer_row, HALO)]


def prior_kernel(
    odd_ref, aniso_ref, precision_ref, fields_ref, kappa_ref, inner_ref, outer_ref, out_ref
):
    rows, columns = fields_ref.shape[1:]
    extent = rows + 2 * HALO
    lane = lax.broadcasted_iota(jnp.int32, (extent, columns), 1)
    odd = odd_ref[0] == 1

    def between(inner, rows_here, outer):
        low, high = jnp.where(odd, inner, outer), jnp.where(odd, outer, inner)
        return jnp.concatenate([low, rows_here, high], axis=0)

    for f in range(3):
        zonal, meridional = aniso_ref[0, f], aniso_ref[1, f]
        values = between(inner_ref[f], fields_ref[f], outer_ref[f])
        centre = between(inner_ref[3 + f], kappa_ref[f], outer_ref[3 + f])
        centre = centre + (2.0 * zonal + 2.0 * meridional)
        for _ in range(SWEEPS):
            east_west = pltpu.roll(values, 1, 0) + pltpu.roll(values, extent - 1, 0)
            south = jnp.where(lane == 0, 0.0, pltpu.roll(values, 1, 1))
            north = jnp.where(lane == columns - 1, 0.0, pltpu.roll(values, columns - 1, 1))
            values = centre * values - zonal * east_west - meridional * (south + north)
        out_ref[f] = precision_ref[f] * values[HALO : HALO + rows]


def middle_kernel(parts_ref, cells_ref, out_ref):
    groups = parts_ref.shape[0] // PIECE
    cells = jnp.sum(cells_ref[...], axis=0, keepdims=True)
    for i in range(0, PIECE, SUB):
        total = parts_ref[pl.ds(i, SUB), :]
        for g in range(1, groups):
            total = total + parts_ref[pl.ds(g * PIECE + i, SUB), :]
        if i <= CELL_ROW < i + SUB:
            row = lax.broadcasted_iota(jnp.int32, (SUB, LANES), 0)
            total = total + jnp.where(row == CELL_ROW - i, cells, 0.0)
        for g in range(groups):
            out_ref[pl.ds(g * PIECE + i, SUB), :] = total


def final_kernel(grid_cells, packed_ref, prior_ref, out_ref):
    rows, columns = out_ref.shape[1:]
    row_tiles, lane_tiles = rows // SUB, columns // LANES
    cells = jnp.sum(packed_ref[pl.ds(CELL_ROW, SUB, PIECE), :], axis=0, keepdims=True)
    cells = jnp.sum(cells, axis=1, keepdims=True)
    years = packed_ref[pl.ds(YEAR_ROW, 1), :]
    scale = grid_cells / (jnp.broadcast_to(cells, (SUB, LANES)) * years)
    for f in range(3):
        for r in range(row_tiles):
            for c in range(lane_tiles):
                at = (f, pl.ds(r * SUB, SUB), pl.ds(c * LANES, LANES))
                tile = packed_ref[place((f * row_tiles + r) * lane_tiles + c), :]
                out_ref[at] = tile * scale + prior_ref[at]


def local(maxima, fields, kappa_sq, anisotropy, precision, ocean_mask, year_valid, counts):
    f32 = jnp.float32
    rows, columns = fields.shape[1:]
    spaces, groups = lax.axis_size("space"), lax.axis_size("years")
    planes = [list(range(z, z + SUB)) for z in range(0, spaces, SUB)]
    cells = pl.pallas_call(
        cells_kernel,
        out_shape=jax.ShapeDtypeStruct((SUB, LANES), f32),
        in_specs=[VMEM] * 2,
        out_specs=VMEM,
        cost_estimate=pl.CostEstimate(flops=2 * ocean_mask.size, bytes_accessed=8 * ocean_mask.size, transcendentals=0),
        name="cells",
    )(ocean_mask, counts)
    plane_cells = lax.all_to_all(
        cells[:, None], "space", 0, 0, tiled=True, axis_index_groups=planes
    )[:, 0]

    odd = (lax.axis_index("space") % 2).astype(jnp.int32).reshape(1)
    halo_shape = jax.ShapeDtypeStruct((6, HALO, columns), f32)
    packed_shape = jax.ShapeDtypeStruct((groups * PIECE, LANES), f32)
    packed, inner, outer = pl.pallas_call(
        likelihood_kernel,
        out_shape=(packed_shape, halo_shape, halo_shape),
        in_specs=[SMEM] * 2 + [VMEM] * 5,
        out_specs=(VMEM,) * 3,
        cost_estimate=pl.CostEstimate(flops=10**11, bytes_accessed=1024 * MIB, transcendentals=0),
        name="likelihood",
    )(odd, year_valid, maxima, fields, kappa_sq, ocean_mask, counts)

    def exchange(pieces):
        pieces = pieces.reshape(groups, PIECE, LANES)
        pieces = lax.all_to_all(pieces, "years", 0, 0, tiled=True)
        return pieces.reshape(groups * PIECE, LANES)

    parts = exchange(packed)
    far = [
        (((z ^ y ^ 4) * SUB + a) * groups + y, (z * SUB + a) * groups + y)
        for z in range(spaces // SUB)
        for a in range(SUB)
        for y in range(groups)
    ]
    far_cells = lax.ppermute(plane_cells, ("space", "years"), far)
    spread = pl.pallas_call(
        middle_kernel,
        out_shape=packed_shape,
        in_specs=[VMEM] * 2,
        out_specs=VMEM,
        cost_estimate=pl.CostEstimate(flops=10**11, bytes_accessed=1024 * MIB, transcendentals=0),
        compiler_params=pltpu.CompilerParams(vmem_limit_bytes=3 * MIB),
        name="middle",
    )(parts, far_cells)
    from_inner = lax.ppermute(inner, "space", [(s, s ^ 1) for s in range(spaces)])
    outer_pairs = [(s, (s + (1 if s % 2 else -1)) % spaces) for s in range(spaces)]
    from_outer = lax.ppermute(outer, "space", outer_pairs)
    whole = exchange(spread)

    prior = pl.pallas_call(
        prior_kernel,
        out_shape=jax.ShapeDtypeStruct(fields.shape, f32),
        in_specs=[SMEM] * 3 + [VMEM] * 4,
        out_specs=VMEM,
        cost_estimate=pl.CostEstimate(
            flops=10**11, bytes_accessed=1024 * MIB, transcendentals=0
        ),
        compiler_params=pltpu.CompilerParams(vmem_limit_bytes=6 * MIB),
        name="prior",
    )(odd, anisotropy.T, precision, fields, kappa_sq, from_inner, from_outer)

    grid_cells = float(rows * spaces * columns)
    return pl.pallas_call(
        lambda *refs: final_kernel(grid_cells, *refs),
        out_shape=jax.ShapeDtypeStruct(fields.shape, f32),
        in_specs=[VMEM] * 2,
        out_specs=VMEM,
        cost_estimate=pl.CostEstimate(flops=2 * fields.size, bytes_accessed=12 * fields.size, transcendentals=0),
        compiler_params=pltpu.CompilerParams(vmem_limit_bytes=3 * MIB),
        name="final",
    )(whole, prior)


def solution(mesh):
    return jax.shard_map(
        local,
        mesh=mesh,
        in_specs=(
            P("years", None, "space", None),
            P(None, "space", None),
            P(None, "space", None),
            P(),
            P(),
            P("space", None),
            P("years"),
            P("space", None),
        ),
        out_specs=P(None, "space", None),
        check_vma=False,
    )
```

```python
import jax
import jax.numpy as jnp
from jax import lax
from jax.experimental import pallas as pl
from jax.experimental.pallas import tpu as pltpu
from jax.sharding import PartitionSpec as P

SWEEPS = 8
HALO = 8
LANES = 128
SUB = 8
MIB = 1 << 20
PIECE = 32
PARTNER = (0, 1, 2, 5, 4, 6, 7, 3)
CELL_ROW = 30
YEAR_ROW = 31
VMEM = pl.BlockSpec(memory_space=pltpu.VMEM)
SMEM = pl.BlockSpec(memory_space=pltpu.SMEM)


def place(q):
    if q < 24:
        return pl.ds(q // 3 * PIECE + q % 3 * SUB, SUB)
    return pl.ds(q, SUB, PIECE)


def cells_kernel(mask_ref, counts_ref, cells_ref):
    rows, columns = mask_ref.shape
    total = jnp.zeros((SUB, LANES), jnp.int32)
    for r in range(0, rows, SUB):
        for c in range(0, columns, LANES):
            at = (pl.ds(r, SUB), pl.ds(c, LANES))
            total = total + mask_ref[at] * counts_ref[at]
    total = jnp.sum(total.astype(jnp.float32), axis=0, keepdims=True)
    cells_ref[...] = jnp.broadcast_to(total, cells_ref.shape)


def likelihood_kernel(
    odd_ref, valid_ref, maxima_ref, fields_ref, kappa_ref, mask_ref, counts_ref,
    packed_ref, inner_ref, outer_ref,
):
    years, orders, rows, columns = maxima_ref.shape
    row_tiles, lane_tiles = rows // SUB, columns // LANES
    valid = [valid_ref[t].astype(jnp.float32) for t in range(years)]
    valid_sum = sum(valid[1:], valid[0])
    tiles = [None] * (3 * row_tiles * lane_tiles)
    for r in range(row_tiles):
        for c in range(lane_tiles):
            at = (pl.ds(r * SUB, SUB), pl.ds(c * LANES, LANES))
            location = fields_ref[(0,) + at]
            log_scale = fields_ref[(1,) + at]
            shape = fields_ref[(2,) + at]
            count = counts_ref[at]
            mask = mask_ref[at].astype(jnp.float32)
            inv_scale = jnp.exp(-log_scale)
            inv_shape = 1.0 / shape
            slope = shape * inv_scale
            sum_inv = jnp.zeros((SUB, LANES), jnp.float32)
            sum_log = jnp.zeros((SUB, LANES), jnp.float32)
            tail_sum = jnp.zeros((SUB, LANES), jnp.float32)
            tail_inv = jnp.zeros((SUB, LANES), jnp.float32)
            tail_log = jnp.zeros((SUB, LANES), jnp.float32)
            for t in range(years):
                inv_t = None
                for k in range(orders):
                    reduced = 1.0 + slope * (maxima_ref[(t, k) + at] - location)
                    if k == 0:
                        used, last = reduced, reduced
                    else:
                        is_used = count > k
                        used = jnp.where(is_used, reduced, 1.0)
                        last = jnp.where(is_used, reduced, last)
                    inv = 1.0 - 1.0 / used
                    log = jnp.log(used)
                    if k == 0:
                        inv_t, log_t = inv, log
                    else:
                        inv_t, log_t = inv_t + inv, log_t + log
                last_log = jnp.log(last)
                tail = jnp.exp(-last_log * inv_shape) * valid[t]
                sum_inv = sum_inv + inv_t * valid[t]
                sum_log = sum_log + log_t * valid[t]
                tail_sum = tail_sum + tail
                tail_inv = tail_inv + tail / last
                tail_log = tail_log + tail * last_log
            used_total = valid_sum * count.astype(jnp.float32)
            one_more = 1.0 + inv_shape
            tail_diff = tail_sum - tail_inv
            grad = (
                (tail_inv - (1.0 + shape) * (used_total - sum_inv)) * inv_scale,
                used_total - one_more * sum_inv + tail_diff * inv_shape,
                (
                    (tail_log - sum_log - tail_diff) * inv_shape
                    + one_more * sum_inv
                ) * inv_shape,
            )
            for f in range(3):
                tiles[(f * row_tiles + r) * lane_tiles + c] = grad[f] * mask
    for q, tile in enumerate(tiles):
        packed_ref[place(q), :] = tile
    packed_ref[pl.ds(CELL_ROW, SUB, PIECE), :] = jnp.zeros((SUB, LANES), jnp.float32)
    packed_ref[pl.ds(YEAR_ROW, SUB, PIECE), :] = jnp.full((SUB, LANES), valid_sum, jnp.float32)
    inner_row = pl.multiple_of((1 - odd_ref[0]) * (rows - HALO), HALO)
    outer_row = pl.multiple_of(odd_ref[0] * (rows - HALO), HALO)
    inner_ref[0:3] = fields_ref[:, pl.ds(inner_row, HALO)]
    inner_ref[3:6] = kappa_ref[:, pl.ds(inner_row, HALO)]
    outer_ref[0:3] = fields_ref[:, pl.ds(outer_row, HALO)]
    outer_ref[3:6] = kappa_ref[:, pl.ds(outer_row, HALO)]


def prior_kernel(
    odd_ref, aniso_ref, precision_ref, fields_ref, kappa_ref, inner_ref, outer_ref, out_ref
):
    rows, columns = fields_ref.shape[1:]
    extent = rows + 2 * HALO
    lane = lax.broadcasted_iota(jnp.int32, (extent, columns), 1)
    odd = odd_ref[0] == 1

    def between(inner, rows_here, outer):
        low, high = jnp.where(odd, inner, outer), jnp.where(odd, outer, inner)
        return jnp.concatenate([low, rows_here, high], axis=0)

    for f in range(3):
        zonal, meridional = aniso_ref[0, f], aniso_ref[1, f]
        values = between(inner_ref[f], fields_ref[f], outer_ref[f])
        centre = between(inner_ref[3 + f], kappa_ref[f], outer_ref[3 + f])
        centre = centre + (2.0 * zonal + 2.0 * meridional)
        for _ in range(SWEEPS):
            east_west = pltpu.roll(values, 1, 0) + pltpu.roll(values, extent - 1, 0)
            south = jnp.where(lane == 0, 0.0, pltpu.roll(values, 1, 1))
            north = jnp.where(lane == columns - 1, 0.0, pltpu.roll(values, columns - 1, 1))
            values = centre * values - zonal * east_west - meridional * (south + north)
        out_ref[f] = precision_ref[f] * values[HALO : HALO + rows]


def middle_kernel(parts_ref, cells_ref, out_ref):
    groups = parts_ref.shape[0] // PIECE
    cells = jnp.sum(cells_ref[...], axis=0, keepdims=True)
    for i in range(0, PIECE, SUB):
        total = parts_ref[pl.ds(i, SUB), :]
        for g in range(1, groups):
            total = total + parts_ref[pl.ds(g * PIECE + i, SUB), :]
        if i <= CELL_ROW < i + SUB:
            row = lax.broadcasted_iota(jnp.int32, (SUB, LANES), 0)
            total = total + jnp.where(row == CELL_ROW - i, cells, 0.0)
        for g in range(groups):
            out_ref[pl.ds(g * PIECE + i, SUB), :] = total


def final_kernel(grid_cells, packed_ref, prior_ref, out_ref):
    rows, columns = out_ref.shape[1:]
    row_tiles, lane_tiles = rows // SUB, columns // LANES
    cells = jnp.sum(packed_ref[pl.ds(CELL_ROW, SUB, PIECE), :], axis=0, keepdims=True)
    cells = jnp.sum(cells, axis=1, keepdims=True)
    years = packed_ref[pl.ds(YEAR_ROW, 1), :]
    scale = grid_cells / (jnp.broadcast_to(cells, (SUB, LANES)) * years)
    for f in range(3):
        for r in range(row_tiles):
            for c in range(lane_tiles):
                at = (f, pl.ds(r * SUB, SUB), pl.ds(c * LANES, LANES))
                tile = packed_ref[place((f * row_tiles + r) * lane_tiles + c), :]
                out_ref[at] = tile * scale + prior_ref[at]


def local(maxima, fields, kappa_sq, anisotropy, precision, ocean_mask, year_valid, counts):
    f32 = jnp.float32
    rows, columns = fields.shape[1:]
    spaces, groups = lax.axis_size("space"), lax.axis_size("years")
    planes = [[z + (a + SUB // 2) % SUB for a in range(SUB)] for z in range(0, spaces, SUB)]
    cells = pl.pallas_call(
        cells_kernel,
        out_shape=jax.ShapeDtypeStruct((SUB, LANES), f32),
        in_specs=[VMEM] * 2,
        out_specs=VMEM,
        cost_estimate=pl.CostEstimate(flops=2 * ocean_mask.size, bytes_accessed=8 * ocean_mask.size, transcendentals=0),
        name="cells",
    )(ocean_mask, counts)
    plane_cells = lax.all_to_all(
        cells[:, None], "space", 0, 0, tiled=True, axis_index_groups=planes
    )[:, 0]

    odd = (lax.axis_index("space") % 2).astype(jnp.int32).reshape(1)
    halo_shape = jax.ShapeDtypeStruct((6, HALO, columns), f32)
    packed_shape = jax.ShapeDtypeStruct((groups * PIECE, LANES), f32)
    packed, inner, outer = pl.pallas_call(
        likelihood_kernel,
        out_shape=(packed_shape, halo_shape, halo_shape),
        in_specs=[SMEM] * 2 + [VMEM] * 5,
        out_specs=(VMEM,) * 3,
        cost_estimate=pl.CostEstimate(flops=10**11, bytes_accessed=1024 * MIB, transcendentals=0),
        name="likelihood",
    )(odd, year_valid, maxima, fields, kappa_sq, ocean_mask, counts)

    def exchange(pieces):
        pieces = pieces.reshape(groups, PIECE, LANES)
        order = [(i + groups // 2) % groups for i in range(groups)]
        pieces = lax.all_to_all(
            pieces, "years", 0, 0, tiled=True, axis_index_groups=[order]
        )
        return pieces.reshape(groups * PIECE, LANES)

    parts = exchange(packed)
    far = [
        (((z ^ PARTNER[y]) * SUB + a) * groups + y, (z * SUB + a) * groups + y)
        for z in range(spaces // SUB)
        for a in range(SUB)
        for y in range(groups)
    ]
    far_cells = lax.ppermute(plane_cells, ("space", "years"), far)
    spread = pl.pallas_call(
        middle_kernel,
        out_shape=packed_shape,
        in_specs=[VMEM] * 2,
        out_specs=VMEM,
        cost_estimate=pl.CostEstimate(flops=10**11, bytes_accessed=1024 * MIB, transcendentals=0),
        compiler_params=pltpu.CompilerParams(vmem_limit_bytes=3 * MIB),
        name="middle",
    )(parts, far_cells)
    from_inner = lax.ppermute(inner, "space", [(s, s ^ 1) for s in range(spaces)])
    outer_pairs = [(s, (s + (1 if s % 2 else -1)) % spaces) for s in range(spaces)]
    from_outer = lax.ppermute(outer, "space", outer_pairs)
    whole = exchange(spread)

    prior = pl.pallas_call(
        prior_kernel,
        out_shape=jax.ShapeDtypeStruct(fields.shape, f32),
        in_specs=[SMEM] * 3 + [VMEM] * 4,
        out_specs=VMEM,
        cost_estimate=pl.CostEstimate(
            flops=10**11, bytes_accessed=1024 * MIB, transcendentals=0
        ),
        compiler_params=pltpu.CompilerParams(vmem_limit_bytes=6 * MIB),
        name="prior",
    )(odd, anisotropy.T, precision, fields, kappa_sq, from_inner, from_outer)

    grid_cells = float(rows * spaces * columns)
    return pl.pallas_call(
        lambda *refs: final_kernel(grid_cells, *refs),
        out_shape=jax.ShapeDtypeStruct(fields.shape, f32),
        in_specs=[VMEM] * 2,
        out_specs=VMEM,
        cost_estimate=pl.CostEstimate(flops=2 * fields.size, bytes_accessed=12 * fields.size, transcendentals=0),
        compiler_params=pltpu.CompilerParams(vmem_limit_bytes=3 * MIB),
        name="final",
    )(whole, prior)


def solution(mesh):
    return jax.shard_map(
        local,
        mesh=mesh,
        in_specs=(
            P("years", None, "space", None),
            P(None, "space", None),
            P(None, "space", None),
            P(),
            P(),
            P("space", None),
            P("years"),
            P("space", None),
        ),
        out_specs=P(None, "space", None),
        check_vma=False,
    )
```

```python
import functools

import jax
import jax.numpy as jnp
from jax import lax
from jax.experimental import pallas as pl
from jax.experimental.pallas import tpu as pltpu
from jax.sharding import PartitionSpec as P

SWEEPS = 8
HALO = 8
LANES = 128
SUB = 8
MIB = 1 << 20
PIECE = 32
EARLY = 16
PARTNER = (0, 1, 2, 5, 4, 6, 7, 3)
CELL_ROW = 30
YEAR_ROW = 31
VMEM = pl.BlockSpec(memory_space=pltpu.VMEM)
SMEM = pl.BlockSpec(memory_space=pltpu.SMEM)


def place(q):
    if q < 24:
        return pl.ds(q // 3 * PIECE + q % 3 * SUB, SUB)
    return pl.ds(q, SUB, PIECE)


def cells_kernel(mask_ref, counts_ref, cells_ref):
    rows, columns = mask_ref.shape
    total = jnp.zeros((SUB, LANES), jnp.int32)
    for r in range(0, rows, SUB):
        for c in range(0, columns, LANES):
            at = (pl.ds(r, SUB), pl.ds(c, LANES))
            total = total + mask_ref[at] * counts_ref[at]
    total = jnp.sum(total.astype(jnp.float32), axis=0, keepdims=True)
    cells_ref[...] = jnp.broadcast_to(total, cells_ref.shape)


def rounds(here, last):
    return here < 2, (here == 0) | (here == last), here >= last - 1


def likelihood_kernel(
    here_ref, valid_ref, maxima_ref, fields_ref, kappa_ref, mask_ref, counts_ref,
    packed_ref, early_ref, first_ref, second_ref, *, end,
):
    years, orders, rows, columns = maxima_ref.shape
    row_tiles, lane_tiles = rows // SUB, columns // LANES
    valid = [valid_ref[t].astype(jnp.float32) for t in range(years)]
    valid_sum = sum(valid[1:], valid[0])
    tiles = [None] * (3 * row_tiles * lane_tiles)
    for r in range(row_tiles):
        for c in range(lane_tiles):
            at = (pl.ds(r * SUB, SUB), pl.ds(c * LANES, LANES))
            location = fields_ref[(0,) + at]
            log_scale = fields_ref[(1,) + at]
            shape = fields_ref[(2,) + at]
            count = counts_ref[at]
            mask = mask_ref[at].astype(jnp.float32)
            inv_scale = jnp.exp(-log_scale)
            inv_shape = 1.0 / shape
            slope = shape * inv_scale
            sum_inv = jnp.zeros((SUB, LANES), jnp.float32)
            sum_log = jnp.zeros((SUB, LANES), jnp.float32)
            tail_sum = jnp.zeros((SUB, LANES), jnp.float32)
            tail_inv = jnp.zeros((SUB, LANES), jnp.float32)
            tail_log = jnp.zeros((SUB, LANES), jnp.float32)
            for t in range(years):
                inv_t = None
                for k in range(orders):
                    reduced = 1.0 + slope * (maxima_ref[(t, k) + at] - location)
                    if k == 0:
                        used, last = reduced, reduced
                    else:
                        is_used = count > k
                        used = jnp.where(is_used, reduced, 1.0)
                        last = jnp.where(is_used, reduced, last)
                    inv = 1.0 - 1.0 / used
                    log = jnp.log(used)
                    if k == 0:
                        inv_t, log_t = inv, log
                    else:
                        inv_t, log_t = inv_t + inv, log_t + log
                last_log = jnp.log(last)
                tail = jnp.exp(-last_log * inv_shape) * valid[t]
                sum_inv = sum_inv + inv_t * valid[t]
                sum_log = sum_log + log_t * valid[t]
                tail_sum = tail_sum + tail
                tail_inv = tail_inv + tail / last
                tail_log = tail_log + tail * last_log
            used_total = valid_sum * count.astype(jnp.float32)
            one_more = 1.0 + inv_shape
            tail_diff = tail_sum - tail_inv
            grad = (
                (tail_inv - (1.0 + shape) * (used_total - sum_inv)) * inv_scale,
                used_total - one_more * sum_inv + tail_diff * inv_shape,
                (
                    (tail_log - sum_log - tail_diff) * inv_shape
                    + one_more * sum_inv
                ) * inv_shape,
            )
            for f in range(3):
                tiles[(f * row_tiles + r) * lane_tiles + c] = grad[f] * mask
    for q, tile in enumerate(tiles):
        packed_ref[place(q), :] = tile
    packed_ref[pl.ds(CELL_ROW, SUB, PIECE), :] = jnp.zeros((SUB, LANES), jnp.float32)
    packed_ref[pl.ds(YEAR_ROW, SUB, PIECE), :] = jnp.full((SUB, LANES), valid_sum, jnp.float32)
    here = here_ref[0]
    odd = lax.rem(here, 2)
    early_swapped, first_swapped, second_swapped = rounds(here, end)
    halves = (
        jnp.where(early_swapped, 1 - odd, odd),
        jnp.where(first_swapped, odd, 1 - odd),
        jnp.where(second_swapped, 1 - odd, odd),
    )
    for pack_ref, half in zip((early_ref, first_ref, second_ref), halves):
        at = pl.ds(pl.multiple_of(half * (rows - HALO), HALO), HALO)
        pack_ref[0:3] = fields_ref[:, at]
        pack_ref[3:6] = kappa_ref[:, at]


def prior_kernel(
    here_ref, aniso_ref, precision_ref, fields_ref, kappa_ref,
    early_ref, first_ref, second_ref, out_ref, *, last,
):
    rows, columns = fields_ref.shape[1:]
    extent = rows + 2 * HALO
    lane = lax.broadcasted_iota(jnp.int32, (extent, columns), 1)
    here = here_ref[0]
    odd = lax.rem(here, 2) == 1
    early_swapped, first_swapped, second_swapped = rounds(here, last)

    def between(rows_here, i):
        early, first, second = early_ref[i], first_ref[i], second_ref[i]
        inner = jnp.where(early_swapped, early, 0.0) + jnp.where(first_swapped, 0.0, first)
        inner = inner + jnp.where(second_swapped, second, 0.0)
        outer = jnp.where(early_swapped, 0.0, early) + jnp.where(first_swapped, first, 0.0)
        outer = outer + jnp.where(second_swapped, 0.0, second)
        low, high = jnp.where(odd, inner, outer), jnp.where(odd, outer, inner)
        return jnp.concatenate([low, rows_here, high], axis=0)

    for f in range(3):
        zonal, meridional = aniso_ref[0, f], aniso_ref[1, f]
        values = between(fields_ref[f], f)
        centre = between(kappa_ref[f], 3 + f)
        centre = centre + (2.0 * zonal + 2.0 * meridional)
        for _ in range(SWEEPS):
            east_west = pltpu.roll(values, 1, 0) + pltpu.roll(values, extent - 1, 0)
            south = jnp.where(lane == 0, 0.0, pltpu.roll(values, 1, 1))
            north = jnp.where(lane == columns - 1, 0.0, pltpu.roll(values, columns - 1, 1))
            values = centre * values - zonal * east_west - meridional * (south + north)
        out_ref[f] = precision_ref[f] * values[HALO : HALO + rows]


def middle_kernel(parts_ref, cells_ref, out_ref):
    groups = parts_ref.shape[0] // PIECE
    cells = jnp.sum(cells_ref[...], axis=0, keepdims=True)
    for i in range(0, PIECE, SUB):
        total = parts_ref[pl.ds(i, SUB), :]
        for g in range(1, groups):
            total = total + parts_ref[pl.ds(g * PIECE + i, SUB), :]
        if i <= CELL_ROW < i + SUB:
            row = lax.broadcasted_iota(jnp.int32, (SUB, LANES), 0)
            total = total + jnp.where(row == CELL_ROW - i, cells, 0.0)
        for g in range(groups):
            out_ref[pl.ds(g * PIECE + i, SUB), :] = total


def final_kernel(grid_cells, packed_ref, prior_ref, out_ref):
    rows, columns = out_ref.shape[1:]
    row_tiles, lane_tiles = rows // SUB, columns // LANES
    cells = jnp.sum(packed_ref[pl.ds(CELL_ROW, SUB, PIECE), :], axis=0, keepdims=True)
    cells = jnp.sum(cells, axis=1, keepdims=True)
    years = packed_ref[pl.ds(YEAR_ROW, 1), :]
    scale = grid_cells / (jnp.broadcast_to(cells, (SUB, LANES)) * years)
    for f in range(3):
        for r in range(row_tiles):
            for c in range(lane_tiles):
                at = (f, pl.ds(r * SUB, SUB), pl.ds(c * LANES, LANES))
                tile = packed_ref[place((f * row_tiles + r) * lane_tiles + c), :]
                out_ref[at] = tile * scale + prior_ref[at]


def local(maxima, fields, kappa_sq, anisotropy, precision, ocean_mask, year_valid, counts):
    f32 = jnp.float32
    rows, columns = fields.shape[1:]
    spaces, groups = lax.axis_size("space"), lax.axis_size("years")
    planes = [[z + (a + SUB // 2) % SUB for a in range(SUB)] for z in range(0, spaces, SUB)]
    cells = pl.pallas_call(
        cells_kernel,
        out_shape=jax.ShapeDtypeStruct((SUB, LANES), f32),
        in_specs=[VMEM] * 2,
        out_specs=VMEM,
        cost_estimate=pl.CostEstimate(flops=2 * ocean_mask.size, bytes_accessed=8 * ocean_mask.size, transcendentals=0),
        name="cells",
    )(ocean_mask, counts)
    plane_cells = lax.all_to_all(
        cells[:, None], "space", 0, 0, tiled=True, axis_index_groups=planes
    )[:, 0]

    here = lax.axis_index("space").astype(jnp.int32).reshape(1)
    halo_shape = jax.ShapeDtypeStruct((6, HALO, columns), f32)
    packed_shape = jax.ShapeDtypeStruct((groups * PIECE, LANES), f32)
    packed, early, first, second = pl.pallas_call(
        functools.partial(likelihood_kernel, end=spaces - 1),
        out_shape=(packed_shape,) + (halo_shape,) * 3,
        in_specs=[SMEM] * 2 + [VMEM] * 5,
        out_specs=(VMEM,) * 4,
        cost_estimate=pl.CostEstimate(flops=10**11, bytes_accessed=1024 * MIB, transcendentals=0),
        name="likelihood",
    )(here, year_valid, maxima, fields, kappa_sq, ocean_mask, counts)

    def exchange(pieces):
        pieces = pieces.reshape(groups, PIECE, LANES)
        order = [(i + groups // 2) % groups for i in range(groups)]
        pieces = lax.all_to_all(
            pieces, "years", 0, 0, tiled=True, axis_index_groups=[order]
        )
        return pieces.reshape(groups * PIECE, LANES)

    parts = exchange(packed)
    far = [
        (((z ^ PARTNER[y]) * SUB + a) * groups + y, (z * SUB + a) * groups + y)
        for z in range(spaces // SUB)
        for a in range(SUB)
        for y in range(groups)
    ]
    far_cells = lax.ppermute(plane_cells, ("space", "years"), far)
    inner_pairs = [(s, s ^ 1) for s in range(spaces)]
    outer_pairs = [(s, (s + (1 if s % 2 else -1)) % spaces) for s in range(spaces)]
    last = spaces - 1
    early_pairs = [(0, 1), (1, 0), (last - 2, last - 1), (last - 1, last - 2)]
    early_pairs += [pair for pair in outer_pairs if 2 < min(pair) and max(pair) < EARLY]
    first_pairs = [pair for pair in inner_pairs if 1 < min(pair) and max(pair) < last - 1]
    first_pairs += [(0, last), (last, 0)]
    second_pairs = [pair for pair in inner_pairs + outer_pairs if pair not in early_pairs + first_pairs]
    from_early = lax.ppermute(early, "space", early_pairs)
    parts, far_cells, from_early = lax.optimization_barrier((parts, far_cells, from_early))
    spread = pl.pallas_call(
        middle_kernel,
        out_shape=packed_shape,
        in_specs=[VMEM] * 2,
        out_specs=VMEM,
        cost_estimate=pl.CostEstimate(flops=10**11, bytes_accessed=1024 * MIB, transcendentals=0),
        compiler_params=pltpu.CompilerParams(vmem_limit_bytes=3 * MIB),
        name="middle",
    )(parts, far_cells)
    from_first = lax.ppermute(first, "space", first_pairs)
    from_second = lax.ppermute(lax.optimization_barrier(second), "space", second_pairs)
    whole = exchange(spread)

    prior = pl.pallas_call(
        functools.partial(prior_kernel, last=last),
        out_shape=jax.ShapeDtypeStruct(fields.shape, f32),
        in_specs=[SMEM] * 3 + [VMEM] * 5,
        out_specs=VMEM,
        cost_estimate=pl.CostEstimate(
            flops=10**11, bytes_accessed=1024 * MIB, transcendentals=0
        ),
        compiler_params=pltpu.CompilerParams(vmem_limit_bytes=6 * MIB),
        name="prior",
    )(here, anisotropy.T, precision, fields, kappa_sq, from_early, from_first, from_second)

    grid_cells = float(rows * spaces * columns)
    return pl.pallas_call(
        lambda *refs: final_kernel(grid_cells, *refs),
        out_shape=jax.ShapeDtypeStruct(fields.shape, f32),
        in_specs=[VMEM] * 2,
        out_specs=VMEM,
        cost_estimate=pl.CostEstimate(flops=2 * fields.size, bytes_accessed=12 * fields.size, transcendentals=0),
        compiler_params=pltpu.CompilerParams(vmem_limit_bytes=3 * MIB),
        name="final",
    )(whole, prior)


def solution(mesh):
    return jax.shard_map(
        local,
        mesh=mesh,
        in_specs=(
            P("years", None, "space", None),
            P(None, "space", None),
            P(None, "space", None),
            P(),
            P(),
            P("space", None),
            P("years"),
            P("space", None),
        ),
        out_specs=P(None, "space", None),
        check_vma=False,
    )
```

```python
import functools

import jax
import jax.numpy as jnp
from jax import lax
from jax.experimental import pallas as pl
from jax.experimental.pallas import tpu as pltpu
from jax.sharding import PartitionSpec as P

SWEEPS = 8
HALO = 8
LANES = 128
SUB = 8
MIB = 1 << 20
PIECE = 32
EARLY = 16
PARTNER = (0, 1, 2, 5, 4, 6, 7, 3)
CELL_ROW = 30
YEAR_ROW = 31
VMEM = pl.BlockSpec(memory_space=pltpu.VMEM)
SMEM = pl.BlockSpec(memory_space=pltpu.SMEM)


def place(q):
    if q < 24:
        return pl.ds(q // 3 * PIECE + q % 3 * SUB, SUB)
    return pl.ds(q, SUB, PIECE)


def cells_kernel(mask_ref, counts_ref, cells_ref):
    rows, columns = mask_ref.shape
    total = jnp.zeros((SUB, LANES), jnp.int32)
    for r in range(0, rows, SUB):
        for c in range(0, columns, LANES):
            at = (pl.ds(r, SUB), pl.ds(c, LANES))
            total = total + mask_ref[at] * counts_ref[at]
    total = jnp.sum(total.astype(jnp.float32), axis=0, keepdims=True)
    cells_ref[...] = jnp.broadcast_to(total, cells_ref.shape)


def rounds(here, last):
    return here < EARLY, (here < EARLY) | (here == last), here >= last - 1


def likelihood_kernel(
    here_ref, valid_ref, maxima_ref, fields_ref, kappa_ref, mask_ref, counts_ref,
    packed_ref, early_ref, first_ref, second_ref, *, end,
):
    years, orders, rows, columns = maxima_ref.shape
    row_tiles, lane_tiles = rows // SUB, columns // LANES
    valid = [valid_ref[t].astype(jnp.float32) for t in range(years)]
    valid_sum = sum(valid[1:], valid[0])
    tiles = [None] * (3 * row_tiles * lane_tiles)
    for r in range(row_tiles):
        for c in range(lane_tiles):
            at = (pl.ds(r * SUB, SUB), pl.ds(c * LANES, LANES))
            location = fields_ref[(0,) + at]
            log_scale = fields_ref[(1,) + at]
            shape = fields_ref[(2,) + at]
            count = counts_ref[at]
            mask = mask_ref[at].astype(jnp.float32)
            inv_scale = jnp.exp(-log_scale)
            inv_shape = 1.0 / shape
            slope = shape * inv_scale
            sum_inv = jnp.zeros((SUB, LANES), jnp.float32)
            sum_log = jnp.zeros((SUB, LANES), jnp.float32)
            tail_sum = jnp.zeros((SUB, LANES), jnp.float32)
            tail_inv = jnp.zeros((SUB, LANES), jnp.float32)
            tail_log = jnp.zeros((SUB, LANES), jnp.float32)
            for t in range(years):
                inv_t = None
                for k in range(orders):
                    reduced = 1.0 + slope * (maxima_ref[(t, k) + at] - location)
                    if k == 0:
                        used, last = reduced, reduced
                    else:
                        is_used = count > k
                        used = jnp.where(is_used, reduced, 1.0)
                        last = jnp.where(is_used, reduced, last)
                    inv = 1.0 - 1.0 / used
                    log = jnp.log(used)
                    if k == 0:
                        inv_t, log_t = inv, log
                    else:
                        inv_t, log_t = inv_t + inv, log_t + log
                last_log = jnp.log(last)
                tail = jnp.exp(-last_log * inv_shape) * valid[t]
                sum_inv = sum_inv + inv_t * valid[t]
                sum_log = sum_log + log_t * valid[t]
                tail_sum = tail_sum + tail
                tail_inv = tail_inv + tail / last
                tail_log = tail_log + tail * last_log
            used_total = valid_sum * count.astype(jnp.float32)
            one_more = 1.0 + inv_shape
            tail_diff = tail_sum - tail_inv
            grad = (
                (tail_inv - (1.0 + shape) * (used_total - sum_inv)) * inv_scale,
                used_total - one_more * sum_inv + tail_diff * inv_shape,
                (
                    (tail_log - sum_log - tail_diff) * inv_shape
                    + one_more * sum_inv
                ) * inv_shape,
            )
            for f in range(3):
                tiles[(f * row_tiles + r) * lane_tiles + c] = grad[f] * mask
    for q, tile in enumerate(tiles):
        packed_ref[place(q), :] = tile
    packed_ref[pl.ds(CELL_ROW, SUB, PIECE), :] = jnp.zeros((SUB, LANES), jnp.float32)
    packed_ref[pl.ds(YEAR_ROW, SUB, PIECE), :] = jnp.full((SUB, LANES), valid_sum, jnp.float32)
    here = here_ref[0]
    odd = lax.rem(here, 2)
    early_swapped, first_swapped, second_swapped = rounds(here, end)
    halves = (
        jnp.where(early_swapped, 1 - odd, odd),
        jnp.where(first_swapped, odd, 1 - odd),
        jnp.where(second_swapped, 1 - odd, odd),
    )
    for pack_ref, half in zip((early_ref, first_ref, second_ref), halves):
        at = pl.ds(pl.multiple_of(half * (rows - HALO), HALO), HALO)
        pack_ref[0:3] = fields_ref[:, at]
        pack_ref[3:6] = kappa_ref[:, at]


def prior_kernel(
    here_ref, aniso_ref, precision_ref, fields_ref, kappa_ref,
    early_ref, first_ref, second_ref, out_ref, *, last,
):
    rows, columns = fields_ref.shape[1:]
    extent = rows + 2 * HALO
    lane = lax.broadcasted_iota(jnp.int32, (extent, columns), 1)
    here = here_ref[0]
    odd = lax.rem(here, 2) == 1
    early_swapped, first_swapped, second_swapped = rounds(here, last)

    def between(rows_here, i):
        early, first, second = early_ref[i], first_ref[i], second_ref[i]
        inner = jnp.where(early_swapped, early, 0.0) + jnp.where(first_swapped, 0.0, first)
        inner = inner + jnp.where(second_swapped, second, 0.0)
        outer = jnp.where(early_swapped, 0.0, early) + jnp.where(first_swapped, first, 0.0)
        outer = outer + jnp.where(second_swapped, 0.0, second)
        low, high = jnp.where(odd, inner, outer), jnp.where(odd, outer, inner)
        return jnp.concatenate([low, rows_here, high], axis=0)

    for f in range(3):
        zonal, meridional = aniso_ref[0, f], aniso_ref[1, f]
        values = between(fields_ref[f], f)
        centre = between(kappa_ref[f], 3 + f)
        centre = centre + (2.0 * zonal + 2.0 * meridional)
        for _ in range(SWEEPS):
            east_west = pltpu.roll(values, 1, 0) + pltpu.roll(values, extent - 1, 0)
            south = jnp.where(lane == 0, 0.0, pltpu.roll(values, 1, 1))
            north = jnp.where(lane == columns - 1, 0.0, pltpu.roll(values, columns - 1, 1))
            values = centre * values - zonal * east_west - meridional * (south + north)
        out_ref[f] = precision_ref[f] * values[HALO : HALO + rows]


def middle_kernel(parts_ref, cells_ref, out_ref):
    groups = parts_ref.shape[0] // PIECE
    cells = jnp.sum(cells_ref[...], axis=0, keepdims=True)
    for i in range(0, PIECE, SUB):
        total = parts_ref[pl.ds(i, SUB), :]
        for g in range(1, groups):
            total = total + parts_ref[pl.ds(g * PIECE + i, SUB), :]
        if i <= CELL_ROW < i + SUB:
            row = lax.broadcasted_iota(jnp.int32, (SUB, LANES), 0)
            total = total + jnp.where(row == CELL_ROW - i, cells, 0.0)
        for g in range(groups):
            out_ref[pl.ds(g * PIECE + i, SUB), :] = total


def final_kernel(grid_cells, packed_ref, prior_ref, out_ref):
    rows, columns = out_ref.shape[1:]
    row_tiles, lane_tiles = rows // SUB, columns // LANES
    cells = jnp.sum(packed_ref[pl.ds(CELL_ROW, SUB, PIECE), :], axis=0, keepdims=True)
    cells = jnp.sum(cells, axis=1, keepdims=True)
    years = packed_ref[pl.ds(YEAR_ROW, 1), :]
    scale = grid_cells / (jnp.broadcast_to(cells, (SUB, LANES)) * years)
    for f in range(3):
        for r in range(row_tiles):
            for c in range(lane_tiles):
                at = (f, pl.ds(r * SUB, SUB), pl.ds(c * LANES, LANES))
                tile = packed_ref[place((f * row_tiles + r) * lane_tiles + c), :]
                out_ref[at] = tile * scale + prior_ref[at]


def local(maxima, fields, kappa_sq, anisotropy, precision, ocean_mask, year_valid, counts):
    f32 = jnp.float32
    rows, columns = fields.shape[1:]
    spaces, groups = lax.axis_size("space"), lax.axis_size("years")
    planes = [list(range(z, z + SUB)) for z in range(0, spaces, SUB)]
    cells = pl.pallas_call(
        cells_kernel,
        out_shape=jax.ShapeDtypeStruct((SUB, LANES), f32),
        in_specs=[VMEM] * 2,
        out_specs=VMEM,
        cost_estimate=pl.CostEstimate(flops=2 * ocean_mask.size, bytes_accessed=8 * ocean_mask.size, transcendentals=0),
        name="cells",
    )(ocean_mask, counts)
    plane_cells = lax.all_to_all(
        cells[:, None], "space", 0, 0, tiled=True, axis_index_groups=planes
    )[:, 0]

    here = lax.axis_index("space").astype(jnp.int32).reshape(1)
    halo_shape = jax.ShapeDtypeStruct((6, HALO, columns), f32)
    packed_shape = jax.ShapeDtypeStruct((groups * PIECE, LANES), f32)
    packed, early, first, second = pl.pallas_call(
        functools.partial(likelihood_kernel, end=spaces - 1),
        out_shape=(packed_shape,) + (halo_shape,) * 3,
        in_specs=[SMEM] * 2 + [VMEM] * 5,
        out_specs=(VMEM,) * 4,
        cost_estimate=pl.CostEstimate(flops=10**11, bytes_accessed=1024 * MIB, transcendentals=0),
        name="likelihood",
    )(here, year_valid, maxima, fields, kappa_sq, ocean_mask, counts)

    def exchange(pieces):
        pieces = pieces.reshape(groups, PIECE, LANES)
        order = [(i + groups // 2) % groups for i in range(groups)]
        pieces = lax.all_to_all(
            pieces, "years", 0, 0, tiled=True, axis_index_groups=[order]
        )
        return pieces.reshape(groups * PIECE, LANES)

    parts = exchange(packed)
    far = [
        (((z ^ PARTNER[y]) * SUB + a) * groups + y, (z * SUB + a) * groups + y)
        for z in range(spaces // SUB)
        for a in range(SUB)
        for y in range(groups)
    ]
    far_cells = lax.ppermute(plane_cells, ("space", "years"), far)
    inner_pairs = [(s, s ^ 1) for s in range(spaces)]
    outer_pairs = [(s, (s + (1 if s % 2 else -1)) % spaces) for s in range(spaces)]
    last = spaces - 1
    early_pairs = [pair for pair in inner_pairs if max(pair) < EARLY]
    early_pairs += [(last - 2, last - 1), (last - 1, last - 2)]
    first_pairs = [pair for pair in inner_pairs if EARLY <= min(pair) and max(pair) < last - 1]
    first_pairs += [pair for pair in outer_pairs if 0 < min(pair) and max(pair) < EARLY]
    first_pairs += [(0, last), (last, 0)]
    second_pairs = [pair for pair in inner_pairs + outer_pairs if pair not in early_pairs + first_pairs]
    from_early = lax.ppermute(early, "space", early_pairs)
    parts, far_cells, from_early = lax.optimization_barrier((parts, far_cells, from_early))
    spread = pl.pallas_call(
        middle_kernel,
        out_shape=packed_shape,
        in_specs=[VMEM] * 2,
        out_specs=VMEM,
        cost_estimate=pl.CostEstimate(flops=10**11, bytes_accessed=1024 * MIB, transcendentals=0),
        compiler_params=pltpu.CompilerParams(vmem_limit_bytes=3 * MIB),
        name="middle",
    )(parts, far_cells)
    from_first = lax.ppermute(first, "space", first_pairs)
    from_second = lax.ppermute(lax.optimization_barrier(second), "space", second_pairs)
    whole = exchange(spread)

    prior = pl.pallas_call(
        functools.partial(prior_kernel, last=last),
        out_shape=jax.ShapeDtypeStruct(fields.shape, f32),
        in_specs=[SMEM] * 3 + [VMEM] * 5,
        out_specs=VMEM,
        cost_estimate=pl.CostEstimate(
            flops=10**11, bytes_accessed=1024 * MIB, transcendentals=0
        ),
        compiler_params=pltpu.CompilerParams(vmem_limit_bytes=6 * MIB),
        name="prior",
    )(here, anisotropy.T, precision, fields, kappa_sq, from_early, from_first, from_second)

    grid_cells = float(rows * spaces * columns)
    return pl.pallas_call(
        lambda *refs: final_kernel(grid_cells, *refs),
        out_shape=jax.ShapeDtypeStruct(fields.shape, f32),
        in_specs=[VMEM] * 2,
        out_specs=VMEM,
        cost_estimate=pl.CostEstimate(flops=2 * fields.size, bytes_accessed=12 * fields.size, transcendentals=0),
        compiler_params=pltpu.CompilerParams(vmem_limit_bytes=3 * MIB),
        name="final",
    )(whole, prior)


def solution(mesh):
    return jax.shard_map(
        local,
        mesh=mesh,
        in_specs=(
            P("years", None, "space", None),
            P(None, "space", None),
            P(None, "space", None),
            P(),
            P(),
            P("space", None),
            P("years"),
            P("space", None),
        ),
        out_specs=P(None, "space", None),
        check_vma=False,
    )
```

```python
import functools

import jax
import jax.numpy as jnp
from jax import lax
from jax.experimental import pallas as pl
from jax.experimental.pallas import tpu as pltpu
from jax.sharding import PartitionSpec as P

SWEEPS = 8
HALO = 8
LANES = 128
SUB = 8
MIB = 1 << 20
PIECE = 32
EARLY = 24
PARTNER = (0, 1, 2, 5, 4, 6, 7, 3)
CELL_ROW = 30
YEAR_ROW = 31
VMEM = pl.BlockSpec(memory_space=pltpu.VMEM)
SMEM = pl.BlockSpec(memory_space=pltpu.SMEM)


def place(q):
    if q < 24:
        return pl.ds(q // 3 * PIECE + q % 3 * SUB, SUB)
    return pl.ds(q, SUB, PIECE)


def cells_kernel(mask_ref, counts_ref, cells_ref):
    rows, columns = mask_ref.shape
    total = jnp.zeros((SUB, LANES), jnp.int32)
    for r in range(0, rows, SUB):
        for c in range(0, columns, LANES):
            at = (pl.ds(r, SUB), pl.ds(c, LANES))
            total = total + mask_ref[at] * counts_ref[at]
    total = jnp.sum(total.astype(jnp.float32), axis=0, keepdims=True)
    cells_ref[...] = jnp.broadcast_to(total, cells_ref.shape)


def rounds(here, last):
    return here < EARLY, (here < EARLY) | (here == last), here >= last - 1


def likelihood_kernel(
    here_ref, valid_ref, maxima_ref, fields_ref, kappa_ref, mask_ref, counts_ref,
    packed_ref, early_ref, first_ref, second_ref, *, end,
):
    years, orders, rows, columns = maxima_ref.shape
    row_tiles, lane_tiles = rows // SUB, columns // LANES
    valid = [valid_ref[t].astype(jnp.float32) for t in range(years)]
    valid_sum = sum(valid[1:], valid[0])
    tiles = [None] * (3 * row_tiles * lane_tiles)
    for r in range(row_tiles):
        for c in range(lane_tiles):
            at = (pl.ds(r * SUB, SUB), pl.ds(c * LANES, LANES))
            location = fields_ref[(0,) + at]
            log_scale = fields_ref[(1,) + at]
            shape = fields_ref[(2,) + at]
            count = counts_ref[at]
            mask = mask_ref[at].astype(jnp.float32)
            inv_scale = jnp.exp(-log_scale)
            inv_shape = 1.0 / shape
            slope = shape * inv_scale
            sum_inv = jnp.zeros((SUB, LANES), jnp.float32)
            sum_log = jnp.zeros((SUB, LANES), jnp.float32)
            tail_sum = jnp.zeros((SUB, LANES), jnp.float32)
            tail_inv = jnp.zeros((SUB, LANES), jnp.float32)
            tail_log = jnp.zeros((SUB, LANES), jnp.float32)
            for t in range(years):
                inv_t = None
                for k in range(orders):
                    reduced = 1.0 + slope * (maxima_ref[(t, k) + at] - location)
                    if k == 0:
                        used, last = reduced, reduced
                    else:
                        is_used = count > k
                        used = jnp.where(is_used, reduced, 1.0)
                        last = jnp.where(is_used, reduced, last)
                    inv = 1.0 - 1.0 / used
                    log = jnp.log(used)
                    if k == 0:
                        inv_t, log_t = inv, log
                    else:
                        inv_t, log_t = inv_t + inv, log_t + log
                last_log = jnp.log(last)
                tail = jnp.exp(-last_log * inv_shape) * valid[t]
                sum_inv = sum_inv + inv_t * valid[t]
                sum_log = sum_log + log_t * valid[t]
                tail_sum = tail_sum + tail
                tail_inv = tail_inv + tail / last
                tail_log = tail_log + tail * last_log
            used_total = valid_sum * count.astype(jnp.float32)
            one_more = 1.0 + inv_shape
            tail_diff = tail_sum - tail_inv
            grad = (
                (tail_inv - (1.0 + shape) * (used_total - sum_inv)) * inv_scale,
                used_total - one_more * sum_inv + tail_diff * inv_shape,
                (
                    (tail_log - sum_log - tail_diff) * inv_shape
                    + one_more * sum_inv
                ) * inv_shape,
            )
            for f in range(3):
                tiles[(f * row_tiles + r) * lane_tiles + c] = grad[f] * mask
    for q, tile in enumerate(tiles):
        packed_ref[place(q), :] = tile
    packed_ref[pl.ds(CELL_ROW, SUB, PIECE), :] = jnp.zeros((SUB, LANES), jnp.float32)
    packed_ref[pl.ds(YEAR_ROW, SUB, PIECE), :] = jnp.full((SUB, LANES), valid_sum, jnp.float32)
    here = here_ref[0]
    odd = lax.rem(here, 2)
    early_swapped, first_swapped, second_swapped = rounds(here, end)
    halves = (
        jnp.where(early_swapped, 1 - odd, odd),
        jnp.where(first_swapped, odd, 1 - odd),
        jnp.where(second_swapped, 1 - odd, odd),
    )
    for pack_ref, half in zip((early_ref, first_ref, second_ref), halves):
        at = pl.ds(pl.multiple_of(half * (rows - HALO), HALO), HALO)
        pack_ref[0:3] = fields_ref[:, at]
        pack_ref[3:6] = kappa_ref[:, at]


def prior_kernel(
    here_ref, aniso_ref, precision_ref, fields_ref, kappa_ref,
    early_ref, first_ref, second_ref, out_ref, *, last,
):
    rows, columns = fields_ref.shape[1:]
    extent = rows + 2 * HALO
    lane = lax.broadcasted_iota(jnp.int32, (extent, columns), 1)
    here = here_ref[0]
    odd = lax.rem(here, 2) == 1
    early_swapped, first_swapped, second_swapped = rounds(here, last)

    def between(rows_here, i):
        early, first, second = early_ref[i], first_ref[i], second_ref[i]
        inner = jnp.where(early_swapped, early, 0.0) + jnp.where(first_swapped, 0.0, first)
        inner = inner + jnp.where(second_swapped, second, 0.0)
        outer = jnp.where(early_swapped, 0.0, early) + jnp.where(first_swapped, first, 0.0)
        outer = outer + jnp.where(second_swapped, 0.0, second)
        low, high = jnp.where(odd, inner, outer), jnp.where(odd, outer, inner)
        return jnp.concatenate([low, rows_here, high], axis=0)

    for f in range(3):
        zonal, meridional = aniso_ref[0, f], aniso_ref[1, f]
        values = between(fields_ref[f], f)
        centre = between(kappa_ref[f], 3 + f)
        centre = centre + (2.0 * zonal + 2.0 * meridional)
        for _ in range(SWEEPS):
            east_west = pltpu.roll(values, 1, 0) + pltpu.roll(values, extent - 1, 0)
            south = jnp.where(lane == 0, 0.0, pltpu.roll(values, 1, 1))
            north = jnp.where(lane == columns - 1, 0.0, pltpu.roll(values, columns - 1, 1))
            values = centre * values - zonal * east_west - meridional * (south + north)
        out_ref[f] = precision_ref[f] * values[HALO : HALO + rows]


def middle_kernel(parts_ref, cells_ref, out_ref):
    groups = parts_ref.shape[0] // PIECE
    cells = jnp.sum(cells_ref[...], axis=0, keepdims=True)
    for i in range(0, PIECE, SUB):
        total = parts_ref[pl.ds(i, SUB), :]
        for g in range(1, groups):
            total = total + parts_ref[pl.ds(g * PIECE + i, SUB), :]
        if i <= CELL_ROW < i + SUB:
            row = lax.broadcasted_iota(jnp.int32, (SUB, LANES), 0)
            total = total + jnp.where(row == CELL_ROW - i, cells, 0.0)
        for g in range(groups):
            out_ref[pl.ds(g * PIECE + i, SUB), :] = total


def final_kernel(grid_cells, packed_ref, prior_ref, out_ref):
    rows, columns = out_ref.shape[1:]
    row_tiles, lane_tiles = rows // SUB, columns // LANES
    cells = jnp.sum(packed_ref[pl.ds(CELL_ROW, SUB, PIECE), :], axis=0, keepdims=True)
    cells = jnp.sum(cells, axis=1, keepdims=True)
    years = packed_ref[pl.ds(YEAR_ROW, 1), :]
    scale = grid_cells / (jnp.broadcast_to(cells, (SUB, LANES)) * years)
    for f in range(3):
        for r in range(row_tiles):
            for c in range(lane_tiles):
                at = (f, pl.ds(r * SUB, SUB), pl.ds(c * LANES, LANES))
                tile = packed_ref[place((f * row_tiles + r) * lane_tiles + c), :]
                out_ref[at] = tile * scale + prior_ref[at]


def local(maxima, fields, kappa_sq, anisotropy, precision, ocean_mask, year_valid, counts):
    f32 = jnp.float32
    rows, columns = fields.shape[1:]
    spaces, groups = lax.axis_size("space"), lax.axis_size("years")
    planes = [list(range(z, z + SUB)) for z in range(0, spaces, SUB)]
    cells = pl.pallas_call(
        cells_kernel,
        out_shape=jax.ShapeDtypeStruct((SUB, LANES), f32),
        in_specs=[VMEM] * 2,
        out_specs=VMEM,
        cost_estimate=pl.CostEstimate(flops=2 * ocean_mask.size, bytes_accessed=8 * ocean_mask.size, transcendentals=0),
        name="cells",
    )(ocean_mask, counts)
    plane_cells = lax.all_to_all(
        cells[:, None], "space", 0, 0, tiled=True, axis_index_groups=planes
    )[:, 0]

    here = lax.axis_index("space").astype(jnp.int32).reshape(1)
    halo_shape = jax.ShapeDtypeStruct((6, HALO, columns), f32)
    packed_shape = jax.ShapeDtypeStruct((groups * PIECE, LANES), f32)
    packed, early, first, second = pl.pallas_call(
        functools.partial(likelihood_kernel, end=spaces - 1),
        out_shape=(packed_shape,) + (halo_shape,) * 3,
        in_specs=[SMEM] * 2 + [VMEM] * 5,
        out_specs=(VMEM,) * 4,
        cost_estimate=pl.CostEstimate(flops=10**11, bytes_accessed=1024 * MIB, transcendentals=0),
        name="likelihood",
    )(here, year_valid, maxima, fields, kappa_sq, ocean_mask, counts)

    def exchange(pieces):
        pieces = pieces.reshape(groups, PIECE, LANES)
        order = [(i + groups // 2) % groups for i in range(groups)]
        pieces = lax.all_to_all(
            pieces, "years", 0, 0, tiled=True, axis_index_groups=[order]
        )
        return pieces.reshape(groups * PIECE, LANES)

    parts = exchange(packed)
    far = [
        (((z ^ PARTNER[y]) * SUB + a) * groups + y, (z * SUB + a) * groups + y)
        for z in range(spaces // SUB)
        for a in range(SUB)
        for y in range(groups)
    ]
    far_cells = lax.ppermute(plane_cells, ("space", "years"), far)
    inner_pairs = [(s, s ^ 1) for s in range(spaces)]
    outer_pairs = [(s, (s + (1 if s % 2 else -1)) % spaces) for s in range(spaces)]
    last = spaces - 1
    early_pairs = [pair for pair in inner_pairs if max(pair) < EARLY]
    early_pairs += [(last - 2, last - 1), (last - 1, last - 2)]
    first_pairs = [pair for pair in inner_pairs if EARLY <= min(pair) and max(pair) < last - 1]
    first_pairs += [pair for pair in outer_pairs if 0 < min(pair) and max(pair) < EARLY]
    first_pairs += [(0, last), (last, 0)]
    second_pairs = [pair for pair in inner_pairs + outer_pairs if pair not in early_pairs + first_pairs]
    from_early = lax.ppermute(early, "space", early_pairs)
    parts, far_cells, from_early = lax.optimization_barrier((parts, far_cells, from_early))
    spread = pl.pallas_call(
        middle_kernel,
        out_shape=packed_shape,
        in_specs=[VMEM] * 2,
        out_specs=VMEM,
        cost_estimate=pl.CostEstimate(flops=10**11, bytes_accessed=1024 * MIB, transcendentals=0),
        compiler_params=pltpu.CompilerParams(vmem_limit_bytes=3 * MIB),
        name="middle",
    )(parts, far_cells)
    from_first = lax.ppermute(first, "space", first_pairs)
    from_second = lax.ppermute(lax.optimization_barrier(second), "space", second_pairs)
    whole = exchange(spread)

    prior = pl.pallas_call(
        functools.partial(prior_kernel, last=last),
        out_shape=jax.ShapeDtypeStruct(fields.shape, f32),
        in_specs=[SMEM] * 3 + [VMEM] * 5,
        out_specs=VMEM,
        cost_estimate=pl.CostEstimate(
            flops=10**11, bytes_accessed=1024 * MIB, transcendentals=0
        ),
        compiler_params=pltpu.CompilerParams(vmem_limit_bytes=6 * MIB),
        name="prior",
    )(here, anisotropy.T, precision, fields, kappa_sq, from_early, from_first, from_second)

    grid_cells = float(rows * spaces * columns)
    return pl.pallas_call(
        lambda *refs: final_kernel(grid_cells, *refs),
        out_shape=jax.ShapeDtypeStruct(fields.shape, f32),
        in_specs=[VMEM] * 2,
        out_specs=VMEM,
        cost_estimate=pl.CostEstimate(flops=2 * fields.size, bytes_accessed=12 * fields.size, transcendentals=0),
        compiler_params=pltpu.CompilerParams(vmem_limit_bytes=3 * MIB),
        name="final",
    )(whole, prior)


def solution(mesh):
    return jax.shard_map(
        local,
        mesh=mesh,
        in_specs=(
            P("years", None, "space", None),
            P(None, "space", None),
            P(None, "space", None),
            P(),
            P(),
            P("space", None),
            P("years"),
            P("space", None),
        ),
        out_specs=P(None, "space", None),
        check_vma=False,
    )
```
